32 devices in a mesh: groups: 2 (over y), context: 4 (over x, core), tensor: 4 (over z).
Axes of the slice: x: 2, y: 2, z: 4, core: 2. Of those that a mesh axis runs over, the one named last changes fastest.
Arguments:
- tokens: bfloat16 [8192, 1920], P(('groups', 'context'), 'tensor'), parts along dimension 0, may hold values from -6 to 6
- in_weight: bfloat16 [1920, 3, 1920], P(None, None, 'tensor'), may hold values from -0.125 to 0.125
- short_filter: bfloat16 [7, 3, 1920], P(None, None, 'tensor'), may hold values from -2 to 2
- mode_weight: float32 [1920, 16], P('tensor'), may hold values from -1.5 to 1.5
- decay_rate: float32 [1920, 16], P('tensor'), as said below
- out_weight: bfloat16 [1920, 1920], P('tensor'), may hold values from -0.1875 to 0.1875
Outputs:
- mixed: bfloat16 [8192, 1920], P(('groups', 'context'), 'tensor'), parts along dimension 0
The draws below stay inside these ranges and needn't reach their ends.
There are 2 independent parts, one for each index of `groups`. The reference program is written for one: setup_inputs(seed, part) draws one part's arguments, and reference() takes and returns one part's arrays. A program takes and returns all parts, laid end to end along the dimension named above; an argument that names none is the same for every part. Nothing has to cross between parts.
Inputs may be any that keep to these rules, and one draw needn't show every extreme that they name: `decay_rate`: every rate lies between 0.2 / 4096 and 1 / 30.
All inputs are finite; a program needn't handle non-finite values.
Results may differ from the reference program's by a relative error of at most 0.025.
Values may be sent and summed in bfloat16 or wider, within the bound.
A program may use at most 64 MiB of HBM per device.

```python
import jax
import jax.numpy as jnp
from jax import lax

D = 1920
MODES = 16
TAPS = 7
L = 4096
N_TENSOR = 4


def draw_decay_rate(key, part):
    first, second, third = jax.random.split(key, 3)
    share = 0.5
    slow_pick = jax.random.uniform(first, (D, MODES), jnp.float32) < share
    slow_log = jax.random.uniform(second, (D, MODES), jnp.float32, jnp.log(0.2 / L), jnp.log(2.0 / L))
    fast_log = jax.random.uniform(third, (D, MODES), jnp.float32, jnp.log(2.0 / L), jnp.log(1.0 / 30.0))
    return jnp.exp(jnp.where(slow_pick, slow_log, fast_log)).astype(jnp.float32)


def with_spikes(result, own_key, source, target, shards_of, factor):
    def block_of(dim):
        return (jnp.arange(result.shape[dim]) // (result.shape[dim] // shards_of)).reshape((-1,) + (1,) * (result.ndim - 1 - dim))

    near = jax.random.permutation(own_key, shards_of)[block_of(target)]
    other_side = (block_of(target) + shards_of // 2) % shards_of
    return jnp.where((block_of(source) == near) | (block_of(source) == other_side), factor * result, result)


def steps_of(stream_key, shape, cuts, least, largest):
    def one(axis_at, parts):
        draws = jax.random.uniform(jax.random.fold_in(jax.random.fold_in(stream_key, 6), axis_at), (parts,), jnp.float32, least / len(cuts), largest / len(cuts))
        return jnp.repeat(jnp.exp(draws), shape[axis_at] // parts).reshape((-1,) + (1,) * (len(shape) - axis_at - 1))

    level = one(*cuts[0])
    for cut in cuts[1:]:
        level = level * one(*cut)
    return level


def gaussian(stream_key, dims, scale, reach, pieces=(), held_as=jnp.bfloat16):
    entries = jax.random.normal(stream_key, dims, jnp.float32) * scale
    if len(pieces) > 0:
        entries = steps_of(stream_key, dims, pieces, -0.22, 0.18) * entries
    return jnp.clip(entries, min=-reach, max=reach).astype(held_as)


def gaussian_with(own_key, extent, deviation, reach, shards, heavy, kind=jnp.bfloat16):
    values = deviation * jax.random.normal(own_key, extent, jnp.float32)
    if shards:
        values = values * steps_of(own_key, extent, shards, -0.22, 0.18)
    return jnp.clip(with_spikes(values, jax.random.fold_in(own_key, 3), *heavy), -reach, reach).astype(kind)


def setup_inputs(seed: int = 0, part: int = 0) -> dict:
    streams_of = jax.random.split(jax.random.key(seed), 7)
    own_keys = jax.random.split(jax.random.fold_in(streams_of[6], part), 7)
    return {
        "tokens": gaussian(own_keys[0], (L, D), 1.0, 6.0, ((0, 4), (1, 4))),
        "in_weight": gaussian(streams_of[1], (D, 3, D), D ** -0.5, 0.125, ((2, 4),)),
        "short_filter": gaussian(streams_of[2], (TAPS, 3, D), 0.4, 2.0, ((2, 4),)),
        "mode_weight": gaussian(streams_of[3], (D, MODES), MODES ** -0.5, 1.5, ((0, 4),), jnp.float32),
        "decay_rate": draw_decay_rate(jax.random.fold_in(streams_of[6], 71), part),
        "out_weight": gaussian_with(streams_of[5], (D, D), D ** -0.5, 0.1875, ((0, 4),), (0, 1, 4, 2.0)),
    }


def reference(tokens, in_weight, short_filter, mode_weight, decay_rate, out_weight):
    proj = jnp.dot(tokens, in_weight.reshape(D, 3 * D), preferred_element_type=jnp.float32)
    proj = proj.reshape(L, 3, D).astype(jnp.bfloat16)
    padded = jnp.concatenate([jnp.zeros((TAPS - 1, 3, D), jnp.bfloat16), proj], 0)
    filtered = jnp.zeros((L, 3, D), jnp.float32)
    for tap_number in range(TAPS):
        begin = TAPS - 1 - tap_number
        filtered = filtered + short_filter[tap_number].astype(jnp.float32)[None] * padded[begin:begin + L].astype(jnp.float32)
    query = filtered[:, 0]
    drive = filtered[:, 1] * filtered[:, 2]
    lags = jnp.arange(L).astype(jnp.float32)
    amplitude = mode_weight * jnp.sqrt(2.0 * decay_rate)
    kernel = jnp.zeros((L, D), jnp.float32)
    for mode_number in range(MODES):
        kernel = kernel + amplitude[:, mode_number][None, :] * jnp.exp(-decay_rate[:, mode_number][None, :] * lags[:, None])
    spectrum = jnp.fft.rfft(drive, n=2 * L, axis=0) * jnp.fft.rfft(kernel, n=2 * L, axis=0)
    conv = jnp.fft.irfft(spectrum, n=2 * L, axis=0)[:L].astype(jnp.float32)
    gated = (query * conv).astype(jnp.bfloat16)
    width = D // N_TENSOR
    total = jnp.zeros((L, D), jnp.float32)
    for group_number in range(N_TENSOR):
        partial_sum = jnp.dot(gated[:, group_number * width:(group_number + 1) * width], out_weight[group_number * width:(group_number + 1) * width], preferred_element_type=jnp.float32).astype(jnp.bfloat16)
        partial_sum = lax.optimization_barrier(partial_sum)
        total = total + partial_sum.astype(jnp.float32)
    return total.astype(jnp.bfloat16)
```

```python
import functools

import jax
import jax.numpy as jnp
from jax import lax
from jax.experimental import pallas as pl
from jax.experimental.pallas import tpu as pltpu
from jax.sharding import PartitionSpec as P

TAPS = 7
HEAD = 8
RIM = 16
MESH = pl.DeviceIdType.MESH


def kernel(
    n, contexts, count, tok, win_hbm, wout_hbm, filt, decay, amp, decay_block, out,
    gathered, rim, win, wout, window, query, drive, gated, state, ends, part, landed,
    local_sem, rim_send, rim_recv, ag_send, ag_recv, end_send, end_recv, rs_send, rs_recv,
):
    rows, ch = tok.shape
    piece = rows // count
    z = lax.axis_index("tensor")
    k = lax.axis_index("context")

    loads = [
        pltpu.make_async_copy(tok, gathered.at[z], local_sem.at[0]),
        pltpu.make_async_copy(win_hbm, win, local_sem.at[1]),
        pltpu.make_async_copy(wout_hbm, wout, local_sem.at[2]),
    ]
    for load in loads:
        load.start()

    barrier = pltpu.get_barrier_semaphore()

    def signal(here, context, tensor):
        @pl.when(here)
        def _():
            pl.semaphore_signal(
                barrier, inc=1, device_id={"context": context, "tensor": tensor}, device_id_type=MESH
            )

    peers = [(z > 0, k, z - 1), (z < n - 1, k, z + 1)]
    for j in range(contexts):
        peers.append((k != j, j, z))
    for step in (-1, 1):
        for zz in range(n):
            peers.append(((k + step >= 0) & (k + step < contexts) & (z != zz), k + step, zz))
    for here, context, tensor in peers:
        signal(here, context, tensor)
    total = functools.reduce(lambda x, y: x + y, [here.astype(jnp.int32) for here, _, _ in peers])
    pl.semaphore_wait(barrier, total)

    def block(c):
        return pl.ds(pl.multiple_of(c * piece, piece), piece)

    def gather_copy(way, src, origin, c):
        side = 0 if way > 0 else 1
        return pltpu.make_async_remote_copy(
            src_ref=src,
            dst_ref=gathered.at[origin, block(c)],
            send_sem=ag_send.at[side, origin, c],
            recv_sem=ag_recv.at[origin, c],
            device_id={"tensor": z + way},
            device_id_type=MESH,
        )

    def send_own(c):
        for way, here in ((1, z < n - 1), (-1, z > 0)):
            @pl.when(here)
            def _():
                gather_copy(way, tok.at[block(c)], z, c).start()

    def rim_copy(slot, zz):
        return pltpu.make_async_remote_copy(
            src_ref=tok.at[pl.ds(rows - RIM, RIM)],
            dst_ref=rim.at[slot],
            send_sem=rim_send.at[zz],
            recv_sem=rim_recv.at[slot],
            device_id={"context": k + 1, "tensor": zz},
            device_id_type=MESH,
        )

    @pl.when(k < contexts - 1)
    def _():
        for zz in range(n):
            rim_copy(z, zz).start()

    send_own(0)
    for load in loads:
        load.wait()
    state[...] = jnp.zeros_like(state)

    def project(stream, load):
        acc = jnp.dot(load(0), win[stream, 0], preferred_element_type=jnp.float32)
        for o in range(1, n):
            acc += jnp.dot(load(o), win[stream, o], preferred_element_type=jnp.float32)
        return acc.astype(jnp.bfloat16).astype(jnp.float32)

    def first_half(c):
        @pl.when((c == 0) & (k == 0))
        def _():
            for stream in range(3):
                window[stream, pl.ds(0, HEAD)] = jnp.zeros((HEAD, ch), jnp.float32)

        @pl.when((c == 0) & (k > 0))
        def _():
            for o in range(n):
                rim_copy(o, 0).wait_recv()
            for stream in range(3):
                window[stream, pl.ds(0, HEAD)] = project(stream, lambda o: rim[o])[RIM - HEAD :]

        for stream in range(3):
            window[stream, pl.ds(HEAD, piece)] = project(stream, lambda o: gathered[o, block(c)])

        def filter_step(r, carry):
            streams = []
            for stream in range(3):
                seen = window[stream, pl.ds(pl.multiple_of(r * 16, 8), 16 + HEAD)]
                total = filt[stream, pl.ds(0, 1)] * seen[HEAD:]
                for tap in range(1, TAPS):
                    total += filt[stream, pl.ds(tap, 1)] * seen[HEAD - tap : HEAD - tap + 16]
                streams.append(total)
            at = pl.ds(pl.multiple_of(c * piece + r * 16, 16), 16)
            query[at] = streams[0]
            drive[at] = streams[1] * streams[2]
            return carry

        lax.fori_loop(0, piece // 16, filter_step, 0)
        for stream in range(3):
            window[stream, pl.ds(0, HEAD)] = window[stream, pl.ds(piece, HEAD)]

        factor = decay[...]

        def state_step(r, now):
            u = drive[pl.ds(pl.multiple_of(c * piece + r * 8, 8), 8)]
            for t in range(8):
                now = now * factor + u[t : t + 1]
            return now

        state[...] = lax.fori_loop(0, piece // 8, state_step, state[...])

    def gather_step(i, carry):
        @pl.when(i + 1 < count)
        def _():
            send_own(i + 1)

        for d in range(n - 1, 0, -1):
            c = i - d
            for way, origin, more in ((1, z - d, z < n - 1), (-1, z + d, z > 0)):
                @pl.when((c >= 0) & (c < count) & (origin >= 0) & (origin < n))
                def _():
                    gather_copy(way, gathered.at[origin, block(c)], origin, c).wait_recv()

                    @pl.when(more)
                    def _():
                        gather_copy(way, gathered.at[origin, block(c)], origin, c).start()

        c = i - (n - 1)

        @pl.when(c >= 0)
        def _():
            first_half(c)

        return carry

    lax.fori_loop(0, count + n - 1, gather_step, 0)

    def end_copy(slot, j):
        return pltpu.make_async_remote_copy(
            src_ref=state,
            dst_ref=ends.at[slot],
            send_sem=end_send.at[j],
            recv_sem=end_recv.at[slot],
            device_id={"context": j},
            device_id_type=MESH,
        )

    for j in range(1, contexts):
        @pl.when(k < j)
        def _():
            end_copy(k, j).start()

    for j in range(1, contexts):
        @pl.when(k < j)
        def _():
            end_copy(k, j).wait_send()

    state[...] = jnp.zeros_like(state)
    for j in range(contexts - 1):
        @pl.when(j < k)
        def _():
            end_copy(j, 0).wait_recv()
            state[...] = state[...] * decay_block[...] + ends[j]

    def second_half(c):
        factor = decay[...]
        weight = amp[...]

        def token_step(r, now):
            at = pl.ds(pl.multiple_of(c * piece + r * 8, 8), 8)
            u = drive[at]
            conv = []
            for t in range(8):
                now = now * factor + u[t : t + 1]
                conv.append(jnp.sum(now * weight, axis=0, keepdims=True))
            gated[pl.ds(pl.multiple_of(r * 8, 8), 8)] = query[at] * jnp.concatenate(conv, axis=0)
            return now

        state[...] = lax.fori_loop(0, piece // 8, token_step, state[...])
        rounded = gated[...].astype(jnp.bfloat16)
        for o in range(n):
            part[o, block(c)] = jnp.dot(
                rounded, wout[o], preferred_element_type=jnp.float32
            ).astype(jnp.bfloat16)

    def sum_copy(way, o, c):
        side = 0 if way > 0 else 1
        return pltpu.make_async_remote_copy(
            src_ref=part.at[o, block(c)],
            dst_ref=landed.at[side, o, block(c)],
            send_sem=rs_send.at[o, c],
            recv_sem=rs_recv.at[side, o, c],
            device_id={"tensor": z + way},
            device_id_type=MESH,
        )

    def sum_step(i, carry):
        @pl.when(i < count)
        def _():
            second_half(i)

        for way, c, first in ((1, i - z, z == 0), (-1, i - (n - 1 - z), z == n - 1)):
            side = 0 if way > 0 else 1
            for o in range(n) if way < 0 else range(n - 1, -1, -1):
                @pl.when((c >= 0) & (c < count) & ((o - z) * way > 0))
                def _():
                    @pl.when(jnp.logical_not(first))
                    def _():
                        sum_copy(way, o, c).wait_recv()
                        part[o, block(c)] = (
                            part[o, block(c)].astype(jnp.float32)
                            + landed[side, o, block(c)].astype(jnp.float32)
                        ).astype(jnp.bfloat16)

                    sum_copy(way, o, c).start()

        c = i - (n - 1)

        @pl.when(c >= 0)
        def _():
            @pl.when(z > 0)
            def _():
                sum_copy(1, z, c).wait_recv()

            @pl.when(z < n - 1)
            def _():
                sum_copy(-1, z, c).wait_recv()

            def own():
                return part[z, block(c)].astype(jnp.float32)

            def arrived(side):
                return landed[side, z, block(c)].astype(jnp.float32)

            @pl.when(z == 0)
            def _():
                out[block(c)] = (own() + arrived(1)).astype(out.dtype)

            @pl.when(z == n - 1)
            def _():
                out[block(c)] = (own() + arrived(0)).astype(out.dtype)

            @pl.when((z > 0) & (z < n - 1))
            def _():
                out[block(c)] = (own() + arrived(0) + arrived(1)).astype(out.dtype)

        return carry

    lax.fori_loop(0, count + n - 1, sum_step, 0)

    @pl.when(k < contexts - 1)
    def _():
        for zz in range(n):
            rim_copy(z, zz).wait_send()

    def drain(c, carry):
        for o in range(n):
            @pl.when((o <= z) & (z < n - 1))
            def _():
                gather_copy(1, gathered.at[o, block(c)], o, c).wait_send()

            @pl.when((o >= z) & (z > 0))
            def _():
                gather_copy(-1, gathered.at[o, block(c)], o, c).wait_send()

            @pl.when(o > z)
            def _():
                sum_copy(1, o, c).wait_send()

            @pl.when(o < z)
            def _():
                sum_copy(-1, o, c).wait_send()

        return carry

    lax.fori_loop(0, count, drain, 0)


def per_device(tokens, in_weight, short_filter, mode_weight, decay_rate, out_weight):
    n = lax.axis_size("tensor")
    contexts = lax.axis_size("context")
    rows, share = tokens.shape
    ch = in_weight.shape[2]
    modes = decay_rate.shape[1]
    count = 8 if rows % 128 == 0 else 1
    piece = rows // count
    win = in_weight.reshape(n, share, 3, ch).transpose(2, 0, 1, 3)
    wout = out_weight.reshape(ch, n, share).transpose(1, 0, 2)
    filt = short_filter.astype(jnp.float32).transpose(1, 0, 2)
    decay = jnp.exp(-decay_rate).T
    decay_block = jnp.exp(-decay_rate * rows).T
    amp = (mode_weight * jnp.sqrt(2.0 * decay_rate)).T
    vmem = pl.BlockSpec(memory_space=pltpu.VMEM)
    anywhere = pl.BlockSpec(memory_space=pl.ANY)
    flops = 2 * rows * n * share * ch * 4
    return pl.pallas_call(
        functools.partial(kernel, n, contexts, count),
        out_shape=jax.ShapeDtypeStruct((rows, share), jnp.bfloat16),
        in_specs=[anywhere] * 3 + [vmem] * 4,
        out_specs=vmem,
        scratch_shapes=[
            pltpu.VMEM((n, rows, share), jnp.bfloat16),
            pltpu.VMEM((n, RIM, share), jnp.bfloat16),
            pltpu.VMEM((3, n, share, ch), jnp.bfloat16),
            pltpu.VMEM((n, ch, share), jnp.bfloat16),
            pltpu.VMEM((3, HEAD + piece, ch), jnp.float32),
            pltpu.VMEM((rows, ch), jnp.float32),
            pltpu.VMEM((rows, ch), jnp.float32),
            pltpu.VMEM((piece, ch), jnp.float32),
            pltpu.VMEM((modes, ch), jnp.float32),
            pltpu.VMEM((contexts, modes, ch), jnp.float32),
            pltpu.VMEM((n, rows, share), jnp.bfloat16),
            pltpu.VMEM((2, n, rows, share), jnp.bfloat16),
            pltpu.SemaphoreType.DMA((3,)),
            pltpu.SemaphoreType.DMA((n,)),
            pltpu.SemaphoreType.DMA((n,)),
            pltpu.SemaphoreType.DMA((2, n, count)),
            pltpu.SemaphoreType.DMA((n, count)),
            pltpu.SemaphoreType.DMA((contexts,)),
            pltpu.SemaphoreType.DMA((contexts,)),
            pltpu.SemaphoreType.DMA((n, count)),
            pltpu.SemaphoreType.DMA((2, n, count)),
        ],
        compiler_params=pltpu.CompilerParams(
            collective_id=0, has_side_effects=True, vmem_limit_bytes=56 * 1024 * 1024
        ),
        cost_estimate=pl.CostEstimate(flops=flops, bytes_accessed=9_000_000, transcendentals=0),
    )(tokens, win, wout, filt, decay, amp, decay_block)


def solution(mesh):
    placed = (
        P(("groups", "context"), "tensor"),
        P(None, None, "tensor"),
        P(None, None, "tensor"),
        P("tensor", None),
        P("tensor", None),
        P("tensor", None),
    )
    return jax.shard_map(
        per_device,
        mesh=mesh,
        in_specs=placed,
        out_specs=P(("groups", "context"), "tensor"),
        check_vma=False,
    )
```

```python
import functools

import jax
import jax.numpy as jnp
from jax import lax
from jax.experimental import pallas as pl
from jax.experimental.pallas import tpu as pltpu
from jax.sharding import PartitionSpec as P

TAPS = 7
HEAD = 8
RIM = 16
MESH = pl.DeviceIdType.MESH


def flip(array):
    height, width = array.shape
    tall, wide = -(-height // 128) * 128, -(-width // 128) * 128
    if wide > width:
        array = jnp.concatenate([array, jnp.zeros((height, wide - width), array.dtype)], 1)
    if tall > height:
        array = jnp.concatenate([array, jnp.zeros((tall - height, wide), array.dtype)], 0)
    return array.T[:width, :height]


def stacked(gathered, c, n):
    share, piece = gathered.shape[2:]
    if share % 16 == 0:
        return gathered[c].reshape(n * share, piece)
    pieces = [gathered[c, o].astype(jnp.float32) for o in range(n)]
    return jnp.concatenate(pieces, 0).astype(jnp.bfloat16)


def kernel(
    n, contexts, count, tok, win_hbm, wout_hbm, filt_in, weight_in, rate, out,
    gathered, tail, rim, win, wout, window, query, drive, gated, state, ends, part, landed,
    filt, decay, amp, decay_block, local_sem, tok_sem, rim_send, rim_recv, ag_send, ag_recv, end_send, end_recv, rs_send, rs_recv,
):
    share, rows = tok.shape
    ch = win.shape[1]
    piece = rows // count
    z = lax.axis_index("tensor")
    k = lax.axis_index("context")

    loads = [
        pltpu.make_async_copy(win_hbm, win, local_sem.at[0]),
        pltpu.make_async_copy(wout_hbm, wout, local_sem.at[1]),
    ]
    own_loads = [
        pltpu.make_async_copy(
            tok.at[:, pl.ds(c * piece, piece)], gathered.at[c, z], tok_sem.at[c]
        )
        for c in range(count)
    ]
    for load in own_loads + loads:
        load.start()

    barrier = pltpu.get_barrier_semaphore()

    def signal(here, context, tensor):
        @pl.when(here)
        def _():
            pl.semaphore_signal(
                barrier, inc=1, device_id={"context": context, "tensor": tensor}, device_id_type=MESH
            )

    peers = [(z > 0, k, z - 1), (z < n - 1, k, z + 1)]
    for j in range(contexts):
        peers.append((k != j, j, z))
    for step in (-1, 1):
        for zz in range(n):
            peers.append(((k + step >= 0) & (k + step < contexts) & (z != zz), k + step, zz))
    for here, context, tensor in peers:
        signal(here, context, tensor)
    total = functools.reduce(lambda x, y: x + y, [here.astype(jnp.int32) for here, _, _ in peers])
    pl.semaphore_wait(barrier, total)

    def block(c):
        return pl.ds(pl.multiple_of(c * piece, piece), piece)

    def gather_copy(way, src, origin, c):
        side = 0 if way > 0 else 1
        return pltpu.make_async_remote_copy(
            src_ref=src,
            dst_ref=gathered.at[c, origin],
            send_sem=ag_send.at[side, origin, c],
            recv_sem=ag_recv.at[origin, c],
            device_id={"tensor": z + way},
            device_id_type=MESH,
        )

    def send_own(c):
        for way, here in ((1, z < n - 1), (-1, z > 0)):
            @pl.when(here)
            def _():
                gather_copy(way, gathered.at[c, z], z, c).start()

    def rim_copy(slot, zz):
        return pltpu.make_async_remote_copy(
            src_ref=tail,
            dst_ref=rim.at[slot],
            send_sem=rim_send.at[zz],
            recv_sem=rim_recv.at[slot],
            device_id={"context": k + 1, "tensor": zz},
            device_id_type=MESH,
        )

    for load in own_loads:
        load.wait()
    send_own(0)

    @pl.when(k < contexts - 1)
    def _():
        tail[...] = flip(gathered[count - 1, z].astype(jnp.float32))[piece - RIM :].astype(tail.dtype)
        for zz in range(n):
            rim_copy(z, zz).start()

    for stream in range(3):
        filt[stream, pl.ds(0, TAPS)] = filt_in[stream].astype(jnp.float32)
    decay[...] = jnp.exp(-rate[...])
    decay_block[...] = jnp.exp(-rate[...] * rows)
    amp[...] = weight_in[...] * jnp.sqrt(2.0 * rate[...])
    state[...] = jnp.zeros_like(state)
    for load in loads:
        load.wait()

    def project(stream, columns):
        acc = jnp.dot(win[stream], columns, preferred_element_type=jnp.float32)
        return flip(acc.astype(jnp.bfloat16).astype(jnp.float32))

    def first_half(c):
        @pl.when((c == 0) & (k == 0))
        def _():
            for stream in range(3):
                window[stream, pl.ds(0, HEAD)] = jnp.zeros((HEAD, ch), jnp.float32)

        @pl.when((c == 0) & (k > 0))
        def _():
            for o in range(n):
                rim_copy(o, 0).wait_recv()
            zeros = jnp.zeros((piece - RIM, share), jnp.float32)
            columns = jnp.concatenate(
                [flip(jnp.concatenate([rim[o].astype(jnp.float32), zeros], 0)) for o in range(n)], 0
            ).astype(jnp.bfloat16)
            for stream in range(3):
                window[stream, pl.ds(0, HEAD)] = project(stream, columns)[RIM - HEAD : RIM]

        columns = stacked(gathered, c, n)
        for stream in range(3):
            window[stream, pl.ds(HEAD, piece)] = project(stream, columns)

        def filter_step(r, carry):
            streams = []
            for stream in range(3):
                seen = window[stream, pl.ds(pl.multiple_of(r * 16, 8), 16 + HEAD)]
                total = filt[stream, pl.ds(0, 1)] * seen[HEAD:]
                for tap in range(1, TAPS):
                    total += filt[stream, pl.ds(tap, 1)] * seen[HEAD - tap : HEAD - tap + 16]
                streams.append(total)
            at = pl.ds(pl.multiple_of(c * piece + r * 16, 16), 16)
            query[at] = streams[0]
            drive[at] = streams[1] * streams[2]
            return carry

        lax.fori_loop(0, piece // 16, filter_step, 0)
        for stream in range(3):
            window[stream, pl.ds(0, HEAD)] = window[stream, pl.ds(piece, HEAD)]

        factor = decay[...]

        def state_step(r, now):
            u = drive[pl.ds(pl.multiple_of(c * piece + r * 8, 8), 8)]
            for t in range(8):
                now = now * factor + u[t : t + 1]
            return now

        state[...] = lax.fori_loop(0, piece // 8, state_step, state[...])

    def gather_step(i, carry):
        @pl.when(i + 1 < count)
        def _():
            send_own(i + 1)

        for d in range(n - 1, 0, -1):
            c = i - d
            for way, origin, more in ((1, z - d, z < n - 1), (-1, z + d, z > 0)):
                @pl.when((c >= 0) & (c < count) & (origin >= 0) & (origin < n))
                def _():
                    gather_copy(way, gathered.at[c, origin], origin, c).wait_recv()

                    @pl.when(more)
                    def _():
                        gather_copy(way, gathered.at[c, origin], origin, c).start()

        c = i - (n - 1)

        @pl.when(c >= 0)
        def _():
            first_half(c)

        return carry

    lax.fori_loop(0, count + n - 1, gather_step, 0)

    def end_copy(slot, j):
        return pltpu.make_async_remote_copy(
            src_ref=state,
            dst_ref=ends.at[slot],
            send_sem=end_send.at[j],
            recv_sem=end_recv.at[slot],
            device_id={"context": j},
            device_id_type=MESH,
        )

    for j in range(1, contexts):
        @pl.when(k < j)
        def _():
            end_copy(k, j).start()

    for j in range(1, contexts):
        @pl.when(k < j)
        def _():
            end_copy(k, j).wait_send()

    state[...] = jnp.zeros_like(state)
    for j in range(contexts - 1):
        @pl.when(j < k)
        def _():
            end_copy(j, 0).wait_recv()
            state[...] = state[...] * decay_block[...] + ends[j]

    def second_half(c):
        factor = decay[...]
        weight = amp[...]

        def token_step(r, now):
            at = pl.ds(pl.multiple_of(c * piece + r * 8, 8), 8)
            u = drive[at]
            conv = []
            for t in range(8):
                now = now * factor + u[t : t + 1]
                conv.append(jnp.sum(now * weight, axis=0, keepdims=True))
            gated[pl.ds(pl.multiple_of(r * 8, 8), 8)] = query[at] * jnp.concatenate(conv, axis=0)
            return now

        state[...] = lax.fori_loop(0, piece // 8, token_step, state[...])
        rounded = gated[...].astype(jnp.bfloat16)
        mixed = flip(jnp.dot(rounded, wout[...], preferred_element_type=jnp.float32))
        for o in range(n):
            part[c, o] = mixed[o * share : (o + 1) * share].astype(jnp.bfloat16)

    def sum_copy(way, o, c):
        side = 0 if way > 0 else 1
        return pltpu.make_async_remote_copy(
            src_ref=part.at[c, o],
            dst_ref=landed.at[side, c, o],
            send_sem=rs_send.at[o, c],
            recv_sem=rs_recv.at[side, o, c],
            device_id={"tensor": z + way},
            device_id_type=MESH,
        )

    def sum_step(i, carry):
        @pl.when(i < count)
        def _():
            second_half(i)

        for way, c, first in ((1, i - z, z == 0), (-1, i - (n - 1 - z), z == n - 1)):
            side = 0 if way > 0 else 1
            for o in range(n) if way < 0 else range(n - 1, -1, -1):
                @pl.when((c >= 0) & (c < count) & ((o - z) * way > 0))
                def _():
                    @pl.when(jnp.logical_not(first))
                    def _():
                        sum_copy(way, o, c).wait_recv()
                        part[c, o] = (
                            part[c, o].astype(jnp.float32)
                            + landed[side, c, o].astype(jnp.float32)
                        ).astype(jnp.bfloat16)

                    sum_copy(way, o, c).start()

        c = i - (n - 1)

        @pl.when(c >= 0)
        def _():
            @pl.when(z > 0)
            def _():
                sum_copy(1, z, c).wait_recv()

            @pl.when(z < n - 1)
            def _():
                sum_copy(-1, z, c).wait_recv()

            def own():
                return part[c, z].astype(jnp.float32)

            def arrived(side):
                return landed[side, c, z].astype(jnp.float32)

            @pl.when(z == 0)
            def _():
                out[:, block(c)] = (own() + arrived(1)).astype(out.dtype)

            @pl.when(z == n - 1)
            def _():
                out[:, block(c)] = (own() + arrived(0)).astype(out.dtype)

            @pl.when((z > 0) & (z < n - 1))
            def _():
                out[:, block(c)] = (own() + arrived(0) + arrived(1)).astype(out.dtype)

        return carry

    lax.fori_loop(0, count + n - 1, sum_step, 0)

    @pl.when(k < contexts - 1)
    def _():
        for zz in range(n):
            rim_copy(z, zz).wait_send()

    def drain(c, carry):
        for o in range(n):
            @pl.when((o <= z) & (z < n - 1))
            def _():
                gather_copy(1, gathered.at[c, o], o, c).wait_send()

            @pl.when((o >= z) & (z > 0))
            def _():
                gather_copy(-1, gathered.at[c, o], o, c).wait_send()

            @pl.when(o > z)
            def _():
                sum_copy(1, o, c).wait_send()

            @pl.when(o < z)
            def _():
                sum_copy(-1, o, c).wait_send()

        return carry

    lax.fori_loop(0, count, drain, 0)


def per_device(tokens, in_weight, short_filter, mode_weight, decay_rate, out_weight):
    n = lax.axis_size("tensor")
    contexts = lax.axis_size("context")
    rows, share = tokens.shape
    ch = in_weight.shape[2]
    modes = decay_rate.shape[1]
    piece = 128
    count = rows // piece
    vmem = pl.BlockSpec(memory_space=pltpu.VMEM)
    anywhere = pl.BlockSpec(memory_space=pl.ANY)
    flops = 2 * rows * n * share * ch * 4
    out = pl.pallas_call(
        functools.partial(kernel, n, contexts, count),
        out_shape=jax.ShapeDtypeStruct((share, rows), jnp.bfloat16),
        in_specs=[anywhere] * 3 + [vmem] * 3,
        out_specs=vmem,
        scratch_shapes=[
            pltpu.VMEM((count, n, share, piece), jnp.bfloat16),
            pltpu.VMEM((RIM, share), jnp.bfloat16),
            pltpu.VMEM((n, RIM, share), jnp.bfloat16),
            pltpu.VMEM((3, ch, n * share), jnp.bfloat16),
            pltpu.VMEM((ch, n * share), jnp.bfloat16),
            pltpu.VMEM((3, HEAD + piece, ch), jnp.float32),
            pltpu.VMEM((rows, ch), jnp.float32),
            pltpu.VMEM((rows, ch), jnp.float32),
            pltpu.VMEM((piece, ch), jnp.float32),
            pltpu.VMEM((modes, ch), jnp.float32),
            pltpu.VMEM((contexts, modes, ch), jnp.float32),
            pltpu.VMEM((count, n, share, piece), jnp.bfloat16),
            pltpu.VMEM((2, count, n, share, piece), jnp.bfloat16),
            pltpu.VMEM((3, 8, ch), jnp.float32),
            pltpu.VMEM((modes, ch), jnp.float32),
            pltpu.VMEM((modes, ch), jnp.float32),
            pltpu.VMEM((modes, ch), jnp.float32),
            pltpu.SemaphoreType.DMA((2,)),
            pltpu.SemaphoreType.DMA((count,)),
            pltpu.SemaphoreType.DMA((n,)),
            pltpu.SemaphoreType.DMA((n,)),
            pltpu.SemaphoreType.DMA((2, n, count)),
            pltpu.SemaphoreType.DMA((n, count)),
            pltpu.SemaphoreType.DMA((contexts,)),
            pltpu.SemaphoreType.DMA((contexts,)),
            pltpu.SemaphoreType.DMA((n, count)),
            pltpu.SemaphoreType.DMA((2, n, count)),
        ],
        compiler_params=pltpu.CompilerParams(
            collective_id=0, has_side_effects=True, vmem_limit_bytes=56 * 1024 * 1024
        ),
        cost_estimate=pl.CostEstimate(flops=flops, bytes_accessed=9_000_000, transcendentals=0),
    )(
        tokens.T,
        in_weight.transpose(1, 2, 0),
        out_weight,
        short_filter.transpose(1, 0, 2),
        mode_weight.T,
        decay_rate.T,
    )
    return out.T


def solution(mesh):
    placed = (
        P(("groups", "context"), "tensor"),
        P(None, None, "tensor"),
        P(None, None, "tensor"),
        P("tensor", None),
        P("tensor", None),
        P("tensor", None),
    )
    return jax.shard_map(
        per_device,
        mesh=mesh,
        in_specs=placed,
        out_specs=P(("groups", "context"), "tensor"),
        check_vma=False,
    )
```

```python
import functools

import jax
import jax.numpy as jnp
from jax import lax
from jax.experimental import pallas as pl
from jax.experimental.pallas import tpu as pltpu
from jax.sharding import PartitionSpec as P

TAPS = 7
HEAD = 8
MESH = pl.DeviceIdType.MESH


def flip(array):
    height, width = array.shape
    tall, wide = -(-height // 128) * 128, -(-width // 128) * 128
    if wide > width:
        array = jnp.concatenate([array, jnp.zeros((height, wide - width), array.dtype)], 1)
    if tall > height:
        array = jnp.concatenate([array, jnp.zeros((tall - height, wide), array.dtype)], 0)
    return array.T[:width, :height]


def stacked(gathered, c, n):
    share, piece = gathered.shape[2:]
    if share % 16 == 0:
        return gathered[c].reshape(n * share, piece)
    pieces = [gathered[c, o].astype(jnp.float32) for o in range(n)]
    return jnp.concatenate(pieces, 0).astype(jnp.bfloat16)


def kernel(
    n, contexts, count, tok, win_hbm, wout_hbm, filt_in, weight_in, rate, out,
    gathered, tails, rims, win, wout, window, query, drive, gated, state, begin, ends, part,
    landed, done, returned, filt, decay, amp, decay_piece,
    local_sem, own_sem, deal_send, deal_recv, rim_send, rim_recv, ag_send, ag_recv,
    end_send, end_recv, rs_send, rs_recv, out_send, out_recv,
):
    share, rows = tok.shape
    ch = win.shape[1]
    piece = rows // count
    z = lax.axis_index("tensor")
    k = lax.axis_index("context")

    loads = [
        pltpu.make_async_copy(win_hbm, win, local_sem.at[0]),
        pltpu.make_async_copy(wout_hbm, wout, local_sem.at[1]),
    ]
    for load in loads:
        load.start()

    barrier = pltpu.get_barrier_semaphore()

    def signal(here, context, tensor):
        @pl.when(here)
        def _():
            pl.semaphore_signal(
                barrier, inc=1, device_id={"context": context, "tensor": tensor}, device_id_type=MESH
            )

    peers = [(z > 0, k, z - 1), (z < n - 1, k, z + 1)]
    for j in range(contexts):
        peers.append((k != j, j, z))
    for here, context, tensor in peers:
        signal(here, context, tensor)
    total = functools.reduce(lambda x, y: x + y, [here.astype(jnp.int32) for here, _, _ in peers])
    pl.semaphore_wait(barrier, total)

    def block(c):
        return pl.ds(pl.multiple_of(c * piece, piece), piece)

    def dealt(c):
        g = k * count + c
        return g % contexts, g // contexts

    def owner(slab):
        g = slab * contexts + k
        return g // count, g % count

    def deal_copy(c, context, slab):
        return pltpu.make_async_remote_copy(
            src_ref=tok.at[:, block(c)],
            dst_ref=gathered.at[slab, z],
            send_sem=deal_send.at[c],
            recv_sem=deal_recv.at[slab],
            device_id={"context": context},
            device_id_type=MESH,
        )

    def own_copy(c, slab):
        return pltpu.make_async_copy(tok.at[:, block(c)], gathered.at[slab, z], own_sem.at[slab])

    for c in range(count):
        context, slab = dealt(c)

        @pl.when(context == k)
        def _():
            own_copy(c, slab).start()

        @pl.when(context != k)
        def _():
            deal_copy(c, context, slab).start()

    def gather_copy(way, origin, c):
        side = 0 if way > 0 else 1
        return pltpu.make_async_remote_copy(
            src_ref=gathered.at[c, origin],
            dst_ref=gathered.at[c, origin],
            send_sem=ag_send.at[side, origin, c],
            recv_sem=ag_recv.at[origin, c],
            device_id={"tensor": z + way},
            device_id_type=MESH,
        )

    def send_own(slab):
        context, c = owner(slab)

        @pl.when(context == k)
        def _():
            own_copy(c, slab).wait()

        @pl.when(context != k)
        def _():
            deal_copy(c, context, slab).wait_recv()

        for way, here in ((1, z < n - 1), (-1, z > 0)):
            @pl.when(here)
            def _():
                gather_copy(way, z, slab).start()

    send_own(0)
    for stream in range(3):
        filt[stream, pl.ds(0, TAPS)] = filt_in[stream].astype(jnp.float32)
    decay[...] = jnp.exp(-rate[...])
    decay_piece[...] = jnp.exp(-rate[...] * piece)
    amp[...] = weight_in[...] * jnp.sqrt(2.0 * rate[...])
    state[...] = jnp.zeros_like(state)
    for load in loads:
        load.wait()

    def rim_copy(c, slab, context):
        return pltpu.make_async_remote_copy(
            src_ref=tails.at[c],
            dst_ref=rims.at[slab],
            send_sem=rim_send.at[c],
            recv_sem=rim_recv.at[slab],
            device_id={"context": context},
            device_id_type=MESH,
        )

    def rim_target(c):
        wraps = (k == contexts - 1).astype(jnp.int32)
        return c + wraps, (k + 1) % contexts

    def project(c):
        columns = stacked(gathered, c, n)
        for stream in range(3):
            acc = jnp.dot(win[stream], columns, preferred_element_type=jnp.float32)
            window[stream, pl.ds(HEAD, piece)] = flip(acc.astype(jnp.bfloat16).astype(jnp.float32))
        for stream in range(3):
            tails[c, stream] = window[stream, pl.ds(piece, HEAD)]
        slab, context = rim_target(c)

        @pl.when(slab < count)
        def _():
            rim_copy(c, slab, context).start()

    def end_copy(c, slot, context):
        return pltpu.make_async_remote_copy(
            src_ref=ends.at[c, slot],
            dst_ref=ends.at[c, slot],
            send_sem=end_send.at[c, context],
            recv_sem=end_recv.at[c, slot],
            device_id={"context": context},
            device_id_type=MESH,
        )

    def first_half(c):
        starts = (c == 0) & (k == 0)

        @pl.when(starts)
        def _():
            for stream in range(3):
                window[stream, pl.ds(0, HEAD)] = jnp.zeros((HEAD, ch), jnp.float32)

        @pl.when(jnp.logical_not(starts))
        def _():
            rim_copy(0, c, 0).wait_recv()
            for stream in range(3):
                window[stream, pl.ds(0, HEAD)] = rims[c, stream]

        def filter_step(r, carry):
            streams = []
            for stream in range(3):
                seen = window[stream, pl.ds(pl.multiple_of(r * 16, 8), 16 + HEAD)]
                total = filt[stream, pl.ds(0, 1)] * seen[HEAD:]
                for tap in range(1, TAPS):
                    total += filt[stream, pl.ds(tap, 1)] * seen[HEAD - tap : HEAD - tap + 16]
                streams.append(total)
            at = pl.ds(pl.multiple_of(c * piece + r * 16, 16), 16)
            query[at] = streams[0]
            drive[at] = streams[1] * streams[2]
            return carry

        lax.fori_loop(0, piece // 16, filter_step, 0)
        factor = decay[...]

        def state_step(r, now):
            u = drive[pl.ds(pl.multiple_of(c * piece + r * 8, 8), 8)]
            for t in range(8):
                now = now * factor + u[t : t + 1]
            return now

        ends[c, k] = lax.fori_loop(0, piece // 8, state_step, jnp.zeros_like(factor))
        for j in range(contexts):
            @pl.when(k != j)
            def _():
                end_copy(c, k, j).start()

    def second_half(c):
        factor = decay[...]
        weight = amp[...]
        for j in range(contexts):
            @pl.when(k != j)
            def _():
                end_copy(c, j, 0).wait_recv()

            @pl.when(k == j)
            def _():
                begin[...] = state[...]

            state[...] = state[...] * decay_piece[...] + ends[c, j]

        def token_step(r, now):
            at = pl.ds(pl.multiple_of(c * piece + r * 8, 8), 8)
            u = drive[at]
            conv = []
            for t in range(8):
                now = now * factor + u[t : t + 1]
                conv.append(jnp.sum(now * weight, axis=0, keepdims=True))
            gated[pl.ds(pl.multiple_of(r * 8, 8), 8)] = query[at] * jnp.concatenate(conv, axis=0)
            return now

        lax.fori_loop(0, piece // 8, token_step, begin[...])
        rounded = gated[...].astype(jnp.bfloat16)
        mixed = flip(jnp.dot(rounded, wout[...], preferred_element_type=jnp.float32))
        for o in range(n):
            part[c, o] = mixed[o * share : (o + 1) * share].astype(jnp.bfloat16)

    def sum_copy(way, o, c):
        side = 0 if way > 0 else 1
        return pltpu.make_async_remote_copy(
            src_ref=part.at[c, o],
            dst_ref=landed.at[side, c, o],
            send_sem=rs_send.at[o, c],
            recv_sem=rs_recv.at[side, o, c],
            device_id={"tensor": z + way},
            device_id_type=MESH,
        )

    def out_copy(slab, context, c):
        return pltpu.make_async_remote_copy(
            src_ref=done.at[slab],
            dst_ref=returned.at[c],
            send_sem=out_send.at[slab],
            recv_sem=out_recv.at[c],
            device_id={"context": context},
            device_id_type=MESH,
        )

    def sums(i):
        for way, c, first in ((1, i - z, z == 0), (-1, i - (n - 1 - z), z == n - 1)):
            side = 0 if way > 0 else 1
            for o in range(n) if way < 0 else range(n - 1, -1, -1):
                @pl.when((c >= 0) & (c < count) & ((o - z) * way > 0))
                def _():
                    @pl.when(jnp.logical_not(first))
                    def _():
                        sum_copy(way, o, c).wait_recv()
                        part[c, o] = (
                            part[c, o].astype(jnp.float32)
                            + landed[side, c, o].astype(jnp.float32)
                        ).astype(jnp.bfloat16)

                    sum_copy(way, o, c).start()

        c = i - (n - 1)

        @pl.when((c >= 0) & (c < count))
        def _():
            @pl.when(z > 0)
            def _():
                sum_copy(1, z, c).wait_recv()

            @pl.when(z < n - 1)
            def _():
                sum_copy(-1, z, c).wait_recv()

            def own():
                return part[c, z].astype(jnp.float32)

            def arrived(side):
                return landed[side, c, z].astype(jnp.float32)

            @pl.when(z == 0)
            def _():
                done[c] = (own() + arrived(1)).astype(out.dtype)

            @pl.when(z == n - 1)
            def _():
                done[c] = (own() + arrived(0)).astype(out.dtype)

            @pl.when((z > 0) & (z < n - 1))
            def _():
                done[c] = (own() + arrived(0) + arrived(1)).astype(out.dtype)

            context, place = owner(c)

            @pl.when(context != k)
            def _():
                out_copy(c, context, place).start()

    def step(i, carry):
        @pl.when(i + 1 < count)
        def _():
            send_own(i + 1)

        for d in range(n - 1, 0, -1):
            c = i - d
            for way, origin, more in ((1, z - d, z < n - 1), (-1, z + d, z > 0)):
                @pl.when((c >= 0) & (c < count) & (origin >= 0) & (origin < n))
                def _():
                    gather_copy(way, origin, c).wait_recv()

                    @pl.when(more)
                    def _():
                        gather_copy(way, origin, c).start()

        ready = i - (n - 1)

        @pl.when((ready >= 0) & (ready < count))
        def _():
            project(ready)

        @pl.when((ready >= 1) & (ready <= count))
        def _():
            second_half(ready - 1)

        @pl.when(ready >= 1)
        def _():
            sums(ready - 1)

        @pl.when((ready >= 0) & (ready < count))
        def _():
            first_half(ready)

        return carry

    lax.fori_loop(0, count + 2 * n - 1, step, 0)

    for c in range(count):
        context, slab = dealt(c)

        @pl.when(context == k)
        def _():
            out[:, pl.ds(c * piece, piece)] = done[slab]

        @pl.when(context != k)
        def _():
            out_copy(slab, context, c).wait_recv()
            out[:, pl.ds(c * piece, piece)] = returned[c]

    def drain(c, carry):
        context, slab = dealt(c)

        @pl.when(context != k)
        def _():
            deal_copy(c, context, slab).wait_send()

        context, place = owner(c)

        @pl.when(context != k)
        def _():
            out_copy(c, context, place).wait_send()

        slab, context = rim_target(c)

        @pl.when(slab < count)
        def _():
            rim_copy(c, slab, context).wait_send()

        for j in range(contexts):
            @pl.when(k != j)
            def _():
                end_copy(c, k, j).wait_send()

        for o in range(n):
            @pl.when((o <= z) & (z < n - 1))
            def _():
                gather_copy(1, o, c).wait_send()

            @pl.when((o >= z) & (z > 0))
            def _():
                gather_copy(-1, o, c).wait_send()

            @pl.when(o > z)
            def _():
                sum_copy(1, o, c).wait_send()

            @pl.when(o < z)
            def _():
                sum_copy(-1, o, c).wait_send()

        return carry

    lax.fori_loop(0, count, drain, 0)


def per_device(tokens, in_weight, short_filter, mode_weight, decay_rate, out_weight):
    n = lax.axis_size("tensor")
    contexts = lax.axis_size("context")
    rows, share = tokens.shape
    ch = in_weight.shape[2]
    modes = decay_rate.shape[1]
    piece = 128
    count = rows // piece
    vmem = pl.BlockSpec(memory_space=pltpu.VMEM)
    anywhere = pl.BlockSpec(memory_space=pl.ANY)
    flops = 2 * rows * n * share * ch * 4
    out = pl.pallas_call(
        functools.partial(kernel, n, contexts, count),
        out_shape=jax.ShapeDtypeStruct((share, rows), jnp.bfloat16),
        in_specs=[anywhere] * 3 + [vmem] * 3,
        out_specs=vmem,
        scratch_shapes=[
            pltpu.VMEM((count, n, share, piece), jnp.bfloat16),
            pltpu.VMEM((count, 3, HEAD, ch), jnp.float32),
            pltpu.VMEM((count, 3, HEAD, ch), jnp.float32),
            pltpu.VMEM((3, ch, n * share), jnp.bfloat16),
            pltpu.VMEM((ch, n * share), jnp.bfloat16),
            pltpu.VMEM((3, HEAD + piece, ch), jnp.float32),
            pltpu.VMEM((rows, ch), jnp.float32),
            pltpu.VMEM((rows, ch), jnp.float32),
            pltpu.VMEM((piece, ch), jnp.float32),
            pltpu.VMEM((modes, ch), jnp.float32),
            pltpu.VMEM((modes, ch), jnp.float32),
            pltpu.VMEM((count, contexts, modes, ch), jnp.float32),
            pltpu.VMEM((count, n, share, piece), jnp.bfloat16),
            pltpu.VMEM((2, count, n, share, piece), jnp.bfloat16),
            pltpu.VMEM((count, share, piece), jnp.bfloat16),
            pltpu.VMEM((count, share, piece), jnp.bfloat16),
            pltpu.VMEM((3, 8, ch), jnp.float32),
            pltpu.VMEM((modes, ch), jnp.float32),
            pltpu.VMEM((modes, ch), jnp.float32),
            pltpu.VMEM((modes, ch), jnp.float32),
            pltpu.SemaphoreType.DMA((2,)),
            pltpu.SemaphoreType.DMA((count,)),
            pltpu.SemaphoreType.DMA((count,)),
            pltpu.SemaphoreType.DMA((count,)),
            pltpu.SemaphoreType.DMA((count,)),
            pltpu.SemaphoreType.DMA((count,)),
            pltpu.SemaphoreType.DMA((2, n, count)),
            pltpu.SemaphoreType.DMA((n, count)),
            pltpu.SemaphoreType.DMA((count, contexts)),
            pltpu.SemaphoreType.DMA((count, contexts)),
            pltpu.SemaphoreType.DMA((n, count)),
            pltpu.SemaphoreType.DMA((2, n, count)),
            pltpu.SemaphoreType.DMA((count,)),
            pltpu.SemaphoreType.DMA((count,)),
        ],
        compiler_params=pltpu.CompilerParams(
            collective_id=0, has_side_effects=True, vmem_limit_bytes=56 * 1024 * 1024
        ),
        cost_estimate=pl.CostEstimate(flops=flops, bytes_accessed=9_000_000, transcendentals=0),
    )(
        tokens.T,
        in_weight.transpose(1, 2, 0),
        out_weight,
        short_filter.transpose(1, 0, 2),
        mode_weight.T,
        decay_rate.T,
    )
    return out.T


def solution(mesh):
    placed = (
        P(("groups", "context"), "tensor"),
        P(None, None, "tensor"),
        P(None, None, "tensor"),
        P("tensor", None),
        P("tensor", None),
        P("tensor", None),
    )
    return jax.shard_map(
        per_device,
        mesh=mesh,
        in_specs=placed,
        out_specs=P(("groups", "context"), "tensor"),
        check_vma=False,
    )
```

```python
import functools

import jax
import jax.numpy as jnp
from jax import lax
from jax.experimental import pallas as pl
from jax.experimental.pallas import tpu as pltpu
from jax.sharding import PartitionSpec as P

TAPS = 7
HEAD = 8
MESH = pl.DeviceIdType.MESH


def flip(array):
    height, width = array.shape
    tall, wide = -(-height // 128) * 128, -(-width // 128) * 128
    if wide > width:
        array = jnp.concatenate([array, jnp.zeros((height, wide - width), array.dtype)], 1)
    if tall > height:
        array = jnp.concatenate([array, jnp.zeros((tall - height, wide), array.dtype)], 0)
    return array.T[:width, :height]


def stacked(gathered, c, n):
    share, piece = gathered.shape[2:]
    if share % 16 == 0:
        return gathered[c].reshape(n * share, piece)
    pieces = [gathered[c, o].astype(jnp.float32) for o in range(n)]
    return jnp.concatenate(pieces, 0).astype(jnp.bfloat16)


def kernel(
    n, contexts, count, tok, win_hbm, wout_hbm, filt_in, weight_in, rate, out,
    gathered, tails, rims, win, wout, window, query, drive, local, carry_table, gated, state, begin, ends, part,
    landed, done, returned, filt, decay, amp, decay_piece,
    local_sem, own_sem, deal_send, deal_recv, rim_send, rim_recv, ag_send, ag_recv,
    end_send, end_recv, rs_send, rs_recv, out_send, out_recv,
):
    share, rows = tok.shape
    ch = win.shape[1]
    piece = rows // count
    z = lax.axis_index("tensor")
    k = lax.axis_index("context")

    loads = [
        pltpu.make_async_copy(win_hbm, win, local_sem.at[0]),
        pltpu.make_async_copy(wout_hbm, wout, local_sem.at[1]),
    ]
    for load in loads:
        load.start()

    barrier = pltpu.get_barrier_semaphore()

    def signal(here, context, tensor):
        @pl.when(here)
        def _():
            pl.semaphore_signal(
                barrier, inc=1, device_id={"context": context, "tensor": tensor}, device_id_type=MESH
            )

    peers = [(z > 0, k, z - 1), (z < n - 1, k, z + 1)]
    for j in range(contexts):
        peers.append((k != j, j, z))
    for here, context, tensor in peers:
        signal(here, context, tensor)
    total = functools.reduce(lambda x, y: x + y, [here.astype(jnp.int32) for here, _, _ in peers])
    pl.semaphore_wait(barrier, total)

    def block(c):
        return pl.ds(pl.multiple_of(c * piece, piece), piece)

    def dealt(c):
        g = k * count + c
        return g % contexts, g // contexts

    def owner(slab):
        g = slab * contexts + k
        return g // count, g % count

    def deal_copy(c, context, slab):
        return pltpu.make_async_remote_copy(
            src_ref=tok.at[:, block(c)],
            dst_ref=gathered.at[slab, z],
            send_sem=deal_send.at[c],
            recv_sem=deal_recv.at[slab],
            device_id={"context": context},
            device_id_type=MESH,
        )

    def own_copy(c, slab):
        return pltpu.make_async_copy(tok.at[:, block(c)], gathered.at[slab, z], own_sem.at[slab])

    for c in range(count):
        context, slab = dealt(c)

        @pl.when(context == k)
        def _():
            own_copy(c, slab).start()

        @pl.when(context != k)
        def _():
            deal_copy(c, context, slab).start()

    def gather_copy(way, origin, c):
        side = 0 if way > 0 else 1
        return pltpu.make_async_remote_copy(
            src_ref=gathered.at[c, origin],
            dst_ref=gathered.at[c, origin],
            send_sem=ag_send.at[side, origin, c],
            recv_sem=ag_recv.at[origin, c],
            device_id={"tensor": z + way},
            device_id_type=MESH,
        )

    def send_own(slab):
        context, c = owner(slab)

        @pl.when(context == k)
        def _():
            own_copy(c, slab).wait()

        @pl.when(context != k)
        def _():
            deal_copy(c, context, slab).wait_recv()

        for way, here in ((1, z < n - 1), (-1, z > 0)):
            @pl.when(here)
            def _():
                gather_copy(way, z, slab).start()

    def prepare():
        for stream in range(3):
            filt[stream, pl.ds(0, TAPS)] = filt_in[stream].astype(jnp.float32)
        decay[...] = jnp.exp(-rate[...])
        decay_piece[...] = jnp.exp(-rate[...] * piece)
        amp[...] = weight_in[...] * jnp.sqrt(2.0 * rate[...])
        state[...] = jnp.zeros_like(state)
        after = (lax.broadcasted_iota(jnp.int32, (piece, ch), 0) + 1).astype(jnp.float32)
        for m in range(rate.shape[0]):
            carry_table[m] = amp[pl.ds(m, 1)] * jnp.exp(-rate[pl.ds(m, 1)] * after)
        for load in loads:
            load.wait()

    def rim_copy(c, slab, context):
        return pltpu.make_async_remote_copy(
            src_ref=tails.at[c],
            dst_ref=rims.at[slab],
            send_sem=rim_send.at[c],
            recv_sem=rim_recv.at[slab],
            device_id={"context": context},
            device_id_type=MESH,
        )

    def rim_target(c):
        wraps = (k == contexts - 1).astype(jnp.int32)
        return c + wraps, (k + 1) % contexts

    def project(c):
        columns = stacked(gathered, c, n)
        for stream in range(3):
            acc = jnp.dot(win[stream], columns, preferred_element_type=jnp.float32)
            window[stream, pl.ds(HEAD, piece)] = flip(acc.astype(jnp.bfloat16)).astype(jnp.float32)
        for stream in range(3):
            tails[c, stream] = window[stream, pl.ds(piece, HEAD)]
        slab, context = rim_target(c)

        @pl.when(slab < count)
        def _():
            rim_copy(c, slab, context).start()

    def end_copy(c, slot, context):
        return pltpu.make_async_remote_copy(
            src_ref=ends.at[c, slot],
            dst_ref=ends.at[c, slot],
            send_sem=end_send.at[c, context],
            recv_sem=end_recv.at[c, slot],
            device_id={"context": context},
            device_id_type=MESH,
        )

    def first_half(c):
        starts = (c == 0) & (k == 0)

        @pl.when(starts)
        def _():
            for stream in range(3):
                window[stream, pl.ds(0, HEAD)] = jnp.zeros((HEAD, ch), jnp.float32)

        @pl.when(jnp.logical_not(starts))
        def _():
            rim_copy(0, c, 0).wait_recv()
            for stream in range(3):
                window[stream, pl.ds(0, HEAD)] = rims[c, stream]

        def filter_step(r, carry):
            streams = []
            for stream in range(3):
                seen = window[stream, pl.ds(pl.multiple_of(r * 16, 8), 16 + HEAD)]
                total = filt[stream, pl.ds(0, 1)] * seen[HEAD:]
                for tap in range(1, TAPS):
                    total += filt[stream, pl.ds(tap, 1)] * seen[HEAD - tap : HEAD - tap + 16]
                streams.append(total)
            at = pl.ds(pl.multiple_of(r * 16, 16), 16)
            query[at] = streams[0]
            drive[at] = streams[1] * streams[2]
            return carry

        lax.fori_loop(0, piece // 16, filter_step, 0)
        factor = decay[...]

        weight = amp[...]

        def token_step(r, now):
            at = pl.ds(pl.multiple_of(r * 8, 8), 8)
            u = drive[at]
            conv = []
            for t in range(8):
                now = now * factor + u[t : t + 1]
                conv.append(jnp.sum(now * weight, axis=0, keepdims=True))
            local[at] = jnp.concatenate(conv, axis=0)
            return now

        ends[c, k] = lax.fori_loop(0, piece // 8, token_step, jnp.zeros_like(factor))
        for j in range(contexts):
            @pl.when(k != j)
            def _():
                end_copy(c, k, j).start()

    def second_half(c):
        for j in range(contexts):
            @pl.when(k != j)
            def _():
                end_copy(c, j, 0).wait_recv()

            @pl.when(k == j)
            def _():
                begin[...] = state[...]

            state[...] = state[...] * decay_piece[...] + ends[c, j]

        def carry_step(r, carry):
            at = pl.ds(pl.multiple_of(r * 32, 32), 32)
            conv = local[at]
            for m in range(begin.shape[0]):
                conv += carry_table[m, at] * begin[pl.ds(m, 1)]
            gated[at] = (query[at] * conv).astype(jnp.bfloat16)
            return carry

        lax.fori_loop(0, piece // 32, carry_step, 0)
        mixed = jnp.dot(gated[...], wout[...], preferred_element_type=jnp.float32)
        mixed = flip(mixed.astype(jnp.bfloat16) if share % 16 == 0 else mixed)
        for o in range(n):
            part[c, o] = mixed[o * share : (o + 1) * share].astype(jnp.bfloat16)

    def sum_copy(way, o, c):
        side = 0 if way > 0 else 1
        return pltpu.make_async_remote_copy(
            src_ref=part.at[c, o],
            dst_ref=landed.at[side, c, o],
            send_sem=rs_send.at[o, c],
            recv_sem=rs_recv.at[side, o, c],
            device_id={"tensor": z + way},
            device_id_type=MESH,
        )

    def out_copy(slab, context, c):
        return pltpu.make_async_remote_copy(
            src_ref=done.at[slab],
            dst_ref=returned.at[c],
            send_sem=out_send.at[slab],
            recv_sem=out_recv.at[c],
            device_id={"context": context},
            device_id_type=MESH,
        )

    def sums(i):
        for way, c, first in ((1, i - z, z == 0), (-1, i - (n - 1 - z), z == n - 1)):
            side = 0 if way > 0 else 1
            for o in range(n) if way < 0 else range(n - 1, -1, -1):
                @pl.when((c >= 0) & (c < count) & ((o - z) * way > 0))
                def _():
                    @pl.when(jnp.logical_not(first))
                    def _():
                        sum_copy(way, o, c).wait_recv()
                        part[c, o] = (
                            part[c, o].astype(jnp.float32)
                            + landed[side, c, o].astype(jnp.float32)
                        ).astype(jnp.bfloat16)

                    sum_copy(way, o, c).start()

        c = i - (n - 1)

        @pl.when((c >= 0) & (c < count))
        def _():
            @pl.when(z > 0)
            def _():
                sum_copy(1, z, c).wait_recv()

            @pl.when(z < n - 1)
            def _():
                sum_copy(-1, z, c).wait_recv()

            def own():
                return part[c, z].astype(jnp.float32)

            def arrived(side):
                return landed[side, c, z].astype(jnp.float32)

            @pl.when(z == 0)
            def _():
                done[c] = (own() + arrived(1)).astype(out.dtype)

            @pl.when(z == n - 1)
            def _():
                done[c] = (own() + arrived(0)).astype(out.dtype)

            @pl.when((z > 0) & (z < n - 1))
            def _():
                done[c] = (own() + arrived(0) + arrived(1)).astype(out.dtype)

            context, place = owner(c)

            @pl.when(context != k)
            def _():
                out_copy(c, context, place).start()

    def step(i, carry):
        for d in range(n - 1, 0, -1):
            c = i - d
            for way, origin, more in ((1, z - d, z < n - 1), (-1, z + d, z > 0)):
                @pl.when((c >= 0) & (c < count) & (origin >= 0) & (origin < n))
                def _():
                    gather_copy(way, origin, c).wait_recv()

                    @pl.when(more)
                    def _():
                        gather_copy(way, origin, c).start()

        @pl.when(i < count)
        def _():
            send_own(i)

        ready = i - (n - 1)

        @pl.when(i == 0)
        def _():
            prepare()

        @pl.when((ready >= 0) & (ready < count))
        def _():
            project(ready)

        @pl.when((ready >= 1) & (ready <= count))
        def _():
            second_half(ready - 1)

        @pl.when(ready >= 1)
        def _():
            sums(ready - 1)

        @pl.when((ready >= 0) & (ready < count))
        def _():
            first_half(ready)

        return carry

    lax.fori_loop(0, count + 2 * n - 1, step, 0)

    for c in range(count):
        context, slab = dealt(c)

        @pl.when(context == k)
        def _():
            out[:, pl.ds(c * piece, piece)] = done[slab]

        @pl.when(context != k)
        def _():
            out_copy(slab, context, c).wait_recv()
            out[:, pl.ds(c * piece, piece)] = returned[c]

    def drain(c, carry):
        context, slab = dealt(c)

        @pl.when(context != k)
        def _():
            deal_copy(c, context, slab).wait_send()

        context, place = owner(c)

        @pl.when(context != k)
        def _():
            out_copy(c, context, place).wait_send()

        slab, context = rim_target(c)

        @pl.when(slab < count)
        def _():
            rim_copy(c, slab, context).wait_send()

        for j in range(contexts):
            @pl.when(k != j)
            def _():
                end_copy(c, k, j).wait_send()

        for o in range(n):
            @pl.when((o <= z) & (z < n - 1))
            def _():
                gather_copy(1, o, c).wait_send()

            @pl.when((o >= z) & (z > 0))
            def _():
                gather_copy(-1, o, c).wait_send()

            @pl.when(o > z)
            def _():
                sum_copy(1, o, c).wait_send()

            @pl.when(o < z)
            def _():
                sum_copy(-1, o, c).wait_send()

        return carry

    lax.fori_loop(0, count, drain, 0)


def per_device(tokens, in_weight, short_filter, mode_weight, decay_rate, out_weight):
    n = lax.axis_size("tensor")
    contexts = lax.axis_size("context")
    rows, share = tokens.shape
    ch = in_weight.shape[2]
    modes = decay_rate.shape[1]
    piece = 128
    count = rows // piece
    vmem = pl.BlockSpec(memory_space=pltpu.VMEM)
    anywhere = pl.BlockSpec(memory_space=pl.ANY)
    flops = 2 * rows * n * share * ch * 4
    out = pl.pallas_call(
        functools.partial(kernel, n, contexts, count),
        out_shape=jax.ShapeDtypeStruct((share, rows), jnp.bfloat16),
        in_specs=[anywhere] * 3 + [vmem] * 3,
        out_specs=vmem,
        scratch_shapes=[
            pltpu.VMEM((count, n, share, piece), jnp.bfloat16),
            pltpu.VMEM((count, 3, HEAD, ch), jnp.float32),
            pltpu.VMEM((count, 3, HEAD, ch), jnp.float32),
            pltpu.VMEM((3, ch, n * share), jnp.bfloat16),
            pltpu.VMEM((ch, n * share), jnp.bfloat16),
            pltpu.VMEM((3, HEAD + piece, ch), jnp.float32),
            pltpu.VMEM((piece, ch), jnp.float32),
            pltpu.VMEM((piece, ch), jnp.float32),
            pltpu.VMEM((piece, ch), jnp.float32),
            pltpu.VMEM((modes, piece, ch), jnp.float32),
            pltpu.VMEM((piece, ch), jnp.bfloat16),
            pltpu.VMEM((modes, ch), jnp.float32),
            pltpu.VMEM((modes, ch), jnp.float32),
            pltpu.VMEM((count, contexts, modes, ch), jnp.float32),
            pltpu.VMEM((count, n, share, piece), jnp.bfloat16),
            pltpu.VMEM((2, count, n, share, piece), jnp.bfloat16),
            pltpu.VMEM((count, share, piece), jnp.bfloat16),
            pltpu.VMEM((count, share, piece), jnp.bfloat16),
            pltpu.VMEM((3, 8, ch), jnp.float32),
            pltpu.VMEM((modes, ch), jnp.float32),
            pltpu.VMEM((modes, ch), jnp.float32),
            pltpu.VMEM((modes, ch), jnp.float32),
            pltpu.SemaphoreType.DMA((2,)),
            pltpu.SemaphoreType.DMA((count,)),
            pltpu.SemaphoreType.DMA((count,)),
            pltpu.SemaphoreType.DMA((count,)),
            pltpu.SemaphoreType.DMA((count,)),
            pltpu.SemaphoreType.DMA((count,)),
            pltpu.SemaphoreType.DMA((2, n, count)),
            pltpu.SemaphoreType.DMA((n, count)),
            pltpu.SemaphoreType.DMA((count, contexts)),
            pltpu.SemaphoreType.DMA((count, contexts)),
            pltpu.SemaphoreType.DMA((n, count)),
            pltpu.SemaphoreType.DMA((2, n, count)),
            pltpu.SemaphoreType.DMA((count,)),
            pltpu.SemaphoreType.DMA((count,)),
        ],
        compiler_params=pltpu.CompilerParams(
            collective_id=0, has_side_effects=True, vmem_limit_bytes=56 * 1024 * 1024
        ),
        cost_estimate=pl.CostEstimate(flops=flops, bytes_accessed=9_000_000, transcendentals=0),
    )(
        tokens.T,
        in_weight.transpose(1, 2, 0),
        out_weight,
        short_filter.transpose(1, 0, 2),
        mode_weight.T,
        decay_rate.T,
    )
    return out.T


def solution(mesh):
    placed = (
        P(("groups", "context"), "tensor"),
        P(None, None, "tensor"),
        P(None, None, "tensor"),
        P("tensor", None),
        P("tensor", None),
        P("tensor", None),
    )
    return jax.shard_map(
        per_device,
        mesh=mesh,
        in_specs=placed,
        out_specs=P(("groups", "context"), "tensor"),
        check_vma=False,
    )
```

```python
import functools

import jax
import jax.numpy as jnp
from jax import lax
from jax.experimental import pallas as pl
from jax.experimental.pallas import tpu as pltpu
from jax.sharding import PartitionSpec as P

TAPS = 7
HEAD = 8
MESH = pl.DeviceIdType.MESH


def flip(array):
    height, width = array.shape
    tall, wide = -(-height // 128) * 128, -(-width // 128) * 128
    if wide > width:
        array = jnp.concatenate([array, jnp.zeros((height, wide - width), array.dtype)], 1)
    if tall > height:
        array = jnp.concatenate([array, jnp.zeros((tall - height, wide), array.dtype)], 0)
    return array.T[:width, :height]


def stacked(gathered, c, n):
    share, piece = gathered.shape[2:]
    if share % 16 == 0:
        return gathered[c].reshape(n * share, piece)
    pieces = [gathered[c, o].astype(jnp.float32) for o in range(n)]
    return jnp.concatenate(pieces, 0).astype(jnp.bfloat16)


def kernel(
    n, contexts, count, tok, win_hbm, wout_hbm, filt_in, weight_in, rate, out,
    gathered, tails, rims, win, wout, window, query, drive, local, carry_table, gated, state, begin, ends, part,
    landed, done, returned, filt, decay, amp, decay_piece,
    local_sem, own_sem, deal_send, deal_recv, rim_send, rim_recv, ag_send, ag_recv,
    end_send, end_recv, rs_send, rs_recv, out_send, out_recv,
):
    share, rows = tok.shape
    ch = win.shape[1]
    piece = rows // count
    z = lax.axis_index("tensor")
    k = lax.axis_index("context")

    loads = [
        pltpu.make_async_copy(win_hbm, win, local_sem.at[0]),
        pltpu.make_async_copy(wout_hbm, wout, local_sem.at[1]),
    ]
    for load in loads:
        load.start()

    barrier = pltpu.get_barrier_semaphore()

    def signal(here, context, tensor):
        @pl.when(here)
        def _():
            pl.semaphore_signal(
                barrier, inc=1, device_id={"context": context, "tensor": tensor}, device_id_type=MESH
            )

    peers = [(z > 0, k, z - 1), (z < n - 1, k, z + 1)]
    for j in range(contexts):
        peers.append((k != j, j, z))
    for here, context, tensor in peers:
        signal(here, context, tensor)
    total = functools.reduce(lambda x, y: x + y, [here.astype(jnp.int32) for here, _, _ in peers])
    pl.semaphore_wait(barrier, total)

    def block(c):
        return pl.ds(pl.multiple_of(c * piece, piece), piece)

    def dealt(c):
        g = k * count + c
        return g % contexts, g // contexts

    def owner(slab):
        g = slab * contexts + k
        return g // count, g % count

    def deal_copy(c, context, slab):
        return pltpu.make_async_remote_copy(
            src_ref=tok.at[:, block(c)],
            dst_ref=gathered.at[slab, z],
            send_sem=deal_send.at[c],
            recv_sem=deal_recv.at[slab],
            device_id={"context": context},
            device_id_type=MESH,
        )

    def own_copy(c, slab):
        return pltpu.make_async_copy(tok.at[:, block(c)], gathered.at[slab, z], own_sem.at[slab])

    for c in range(count):
        context, slab = dealt(c)

        @pl.when(context == k)
        def _():
            own_copy(c, slab).start()

        @pl.when(context != k)
        def _():
            deal_copy(c, context, slab).start()

    def gather_copy(way, origin, c):
        side = 0 if way > 0 else 1
        return pltpu.make_async_remote_copy(
            src_ref=gathered.at[c, origin],
            dst_ref=gathered.at[c, origin],
            send_sem=ag_send.at[side, origin, c],
            recv_sem=ag_recv.at[origin, c],
            device_id={"tensor": z + way},
            device_id_type=MESH,
        )

    def send_own(slab):
        context, c = owner(slab)

        @pl.when(context == k)
        def _():
            own_copy(c, slab).wait()

        @pl.when(context != k)
        def _():
            deal_copy(c, context, slab).wait_recv()

        for way, here in ((1, z < n - 1), (-1, z > 0)):
            @pl.when(here)
            def _():
                gather_copy(way, z, slab).start()

    def prepare():
        for stream in range(3):
            filt[stream, pl.ds(0, TAPS)] = filt_in[stream].astype(jnp.float32)
        decay[...] = jnp.exp(-rate[...])
        decay_piece[...] = jnp.exp(-rate[...] * piece)
        amp[...] = weight_in[...] * jnp.sqrt(2.0 * rate[...])
        state[...] = jnp.zeros_like(state)
        after = (lax.broadcasted_iota(jnp.int32, (piece, ch), 0) + 1).astype(jnp.float32)
        for m in range(rate.shape[0]):
            carry_table[m] = amp[pl.ds(m, 1)] * jnp.exp(-rate[pl.ds(m, 1)] * after)
        for load in loads:
            load.wait()

    def rim_copy(c, slab, context):
        return pltpu.make_async_remote_copy(
            src_ref=tails.at[c],
            dst_ref=rims.at[slab],
            send_sem=rim_send.at[c],
            recv_sem=rim_recv.at[slab],
            device_id={"context": context},
            device_id_type=MESH,
        )

    def rim_target(c):
        wraps = (k == contexts - 1).astype(jnp.int32)
        return c + wraps, (k + 1) % contexts

    def project(c):
        columns = stacked(gathered, c, n)
        for stream in range(3):
            acc = jnp.dot(win[stream], columns, preferred_element_type=jnp.float32)
            window[stream, pl.ds(HEAD, piece)] = flip(acc.astype(jnp.bfloat16)).astype(jnp.float32)
        for stream in range(3):
            tails[c, stream] = window[stream, pl.ds(piece, HEAD)]
        slab, context = rim_target(c)

        @pl.when(slab < count)
        def _():
            rim_copy(c, slab, context).start()

    def end_copy(c, slot, context):
        return pltpu.make_async_remote_copy(
            src_ref=ends.at[c, slot],
            dst_ref=ends.at[c, slot],
            send_sem=end_send.at[c, context],
            recv_sem=end_recv.at[c, slot],
            device_id={"context": context},
            device_id_type=MESH,
        )

    def first_half(c):
        starts = (c == 0) & (k == 0)

        @pl.when(starts)
        def _():
            for stream in range(3):
                window[stream, pl.ds(0, HEAD)] = jnp.zeros((HEAD, ch), jnp.float32)

        @pl.when(jnp.logical_not(starts))
        def _():
            rim_copy(0, c, 0).wait_recv()
            for stream in range(3):
                window[stream, pl.ds(0, HEAD)] = rims[c, stream]

        def filter_step(r, carry):
            streams = []
            for stream in range(3):
                seen = window[stream, pl.ds(pl.multiple_of(r * 16, 8), 16 + HEAD)]
                total = filt[stream, pl.ds(0, 1)] * seen[HEAD:]
                for tap in range(1, TAPS):
                    total += filt[stream, pl.ds(tap, 1)] * seen[HEAD - tap : HEAD - tap + 16]
                streams.append(total)
            at = pl.ds(pl.multiple_of(r * 16, 16), 16)
            query[at] = streams[0]
            drive[at] = streams[1] * streams[2]
            return carry

        lax.fori_loop(0, piece // 16, filter_step, 0)
        factor = decay[...]

        weight = amp[...]

        def token_step(r, now):
            at = pl.ds(pl.multiple_of(r * 8, 8), 8)
            u = drive[at]
            conv = []
            for t in range(8):
                now = now * factor + u[t : t + 1]
                conv.append(jnp.sum(now * weight, axis=0, keepdims=True))
            local[at] = jnp.concatenate(conv, axis=0)
            return now

        ends[c, k] = lax.fori_loop(0, piece // 8, token_step, jnp.zeros_like(factor))
        for j in range(contexts):
            @pl.when(k != j)
            def _():
                end_copy(c, k, j).start()

    def second_half(c):
        for j in range(contexts):
            @pl.when(k != j)
            def _():
                end_copy(c, j, 0).wait_recv()

            @pl.when(k == j)
            def _():
                begin[...] = state[...]

            state[...] = state[...] * decay_piece[...] + ends[c, j]

        def carry_step(r, carry):
            at = pl.ds(pl.multiple_of(r * 32, 32), 32)
            conv = local[at]
            for m in range(begin.shape[0]):
                conv += carry_table[m, at] * begin[pl.ds(m, 1)]
            gated[at] = (query[at] * conv).astype(jnp.bfloat16)
            return carry

        lax.fori_loop(0, piece // 32, carry_step, 0)
        mixed = jnp.dot(gated[...], wout[...], preferred_element_type=jnp.float32)
        mixed = flip(mixed.astype(jnp.bfloat16) if share % 16 == 0 else mixed)
        for o in range(n):
            part[c, o] = mixed[o * share : (o + 1) * share].astype(jnp.bfloat16)

    def sum_copy(way, o, c):
        side = 0 if way > 0 else 1
        return pltpu.make_async_remote_copy(
            src_ref=part.at[c, o],
            dst_ref=landed.at[side, c, o],
            send_sem=rs_send.at[o, c],
            recv_sem=rs_recv.at[side, o, c],
            device_id={"tensor": z + way},
            device_id_type=MESH,
        )

    def out_copy(slab, context, c):
        return pltpu.make_async_remote_copy(
            src_ref=done.at[slab],
            dst_ref=returned.at[c],
            send_sem=out_send.at[slab],
            recv_sem=out_recv.at[c],
            device_id={"context": context},
            device_id_type=MESH,
        )

    def sums(i):
        for way, c, first in ((1, i - z, z == 0), (-1, i - (n - 1 - z), z == n - 1)):
            side = 0 if way > 0 else 1
            for o in range(n) if way < 0 else range(n - 1, -1, -1):
                @pl.when((c >= 0) & (c < count) & ((o - z) * way > 0))
                def _():
                    @pl.when(jnp.logical_not(first))
                    def _():
                        sum_copy(way, o, c).wait_recv()
                        part[c, o] = (
                            part[c, o].astype(jnp.float32)
                            + landed[side, c, o].astype(jnp.float32)
                        ).astype(jnp.bfloat16)

                    sum_copy(way, o, c).start()

        c = i - (n - 1)

        @pl.when((c >= 0) & (c < count))
        def _():
            @pl.when(z > 0)
            def _():
                sum_copy(1, z, c).wait_recv()

            @pl.when(z < n - 1)
            def _():
                sum_copy(-1, z, c).wait_recv()

            def own():
                return part[c, z].astype(jnp.float32)

            def arrived(side):
                return landed[side, c, z].astype(jnp.float32)

            @pl.when(z == 0)
            def _():
                done[c] = (own() + arrived(1)).astype(out.dtype)

            @pl.when(z == n - 1)
            def _():
                done[c] = (own() + arrived(0)).astype(out.dtype)

            @pl.when((z > 0) & (z < n - 1))
            def _():
                done[c] = (own() + arrived(0) + arrived(1)).astype(out.dtype)

            context, place = owner(c)

            @pl.when(context != k)
            def _():
                out_copy(c, context, place).start()

    def step(i, carry):
        for d in range(n - 1, 0, -1):
            c = i - d
            for way, origin, more in ((1, z - d, z < n - 1), (-1, z + d, z > 0)):
                @pl.when((c >= 0) & (c < count) & (origin >= 0) & (origin < n))
                def _():
                    gather_copy(way, origin, c).wait_recv()

                    @pl.when(more)
                    def _():
                        gather_copy(way, origin, c).start()

        @pl.when(i <= 1)
        def _():
            send_own(i)

        @pl.when((i >= 1) & (i + 1 < count))
        def _():
            send_own(i + 1)

        ready = i - (n - 1)

        @pl.when(i == 0)
        def _():
            prepare()

        @pl.when((ready >= 0) & (ready < count))
        def _():
            project(ready)

        @pl.when((ready >= 1) & (ready <= count))
        def _():
            second_half(ready - 1)

        @pl.when(ready >= 1)
        def _():
            sums(ready - 1)

        @pl.when((ready >= 0) & (ready < count))
        def _():
            first_half(ready)

        return carry

    lax.fori_loop(0, count + 2 * n - 1, step, 0)

    for c in range(count):
        context, slab = dealt(c)

        @pl.when(context == k)
        def _():
            out[:, pl.ds(c * piece, piece)] = done[slab]

        @pl.when(context != k)
        def _():
            out_copy(slab, context, c).wait_recv()
            out[:, pl.ds(c * piece, piece)] = returned[c]

    def drain(c, carry):
        context, slab = dealt(c)

        @pl.when(context != k)
        def _():
            deal_copy(c, context, slab).wait_send()

        context, place = owner(c)

        @pl.when(context != k)
        def _():
            out_copy(c, context, place).wait_send()

        slab, context = rim_target(c)

        @pl.when(slab < count)
        def _():
            rim_copy(c, slab, context).wait_send()

        for j in range(contexts):
            @pl.when(k != j)
            def _():
                end_copy(c, k, j).wait_send()

        for o in range(n):
            @pl.when((o <= z) & (z < n - 1))
            def _():
                gather_copy(1, o, c).wait_send()

            @pl.when((o >= z) & (z > 0))
            def _():
                gather_copy(-1, o, c).wait_send()

            @pl.when(o > z)
            def _():
                sum_copy(1, o, c).wait_send()

            @pl.when(o < z)
            def _():
                sum_copy(-1, o, c).wait_send()

        return carry

    lax.fori_loop(0, count, drain, 0)


def per_device(tokens, in_weight, short_filter, mode_weight, decay_rate, out_weight):
    n = lax.axis_size("tensor")
    contexts = lax.axis_size("context")
    rows, share = tokens.shape
    ch = in_weight.shape[2]
    modes = decay_rate.shape[1]
    piece = 128
    count = rows // piece
    vmem = pl.BlockSpec(memory_space=pltpu.VMEM)
    anywhere = pl.BlockSpec(memory_space=pl.ANY)
    flops = 2 * rows * n * share * ch * 4
    out = pl.pallas_call(
        functools.partial(kernel, n, contexts, count),
        out_shape=jax.ShapeDtypeStruct((share, rows), jnp.bfloat16),
        in_specs=[anywhere] * 3 + [vmem] * 3,
        out_specs=vmem,
        scratch_shapes=[
            pltpu.VMEM((count, n, share, piece), jnp.bfloat16),
            pltpu.VMEM((count, 3, HEAD, ch), jnp.float32),
            pltpu.VMEM((count, 3, HEAD, ch), jnp.float32),
            pltpu.VMEM((3, ch, n * share), jnp.bfloat16),
            pltpu.VMEM((ch, n * share), jnp.bfloat16),
            pltpu.VMEM((3, HEAD + piece, ch), jnp.float32),
            pltpu.VMEM((piece, ch), jnp.float32),
            pltpu.VMEM((piece, ch), jnp.float32),
            pltpu.VMEM((piece, ch), jnp.float32),
            pltpu.VMEM((modes, piece, ch), jnp.float32),
            pltpu.VMEM((piece, ch), jnp.bfloat16),
            pltpu.VMEM((modes, ch), jnp.float32),
            pltpu.VMEM((modes, ch), jnp.float32),
            pltpu.VMEM((count, contexts, modes, ch), jnp.float32),
            pltpu.VMEM((count, n, share, piece), jnp.bfloat16),
            pltpu.VMEM((2, count, n, share, piece), jnp.bfloat16),
            pltpu.VMEM((count, share, piece), jnp.bfloat16),
            pltpu.VMEM((count, share, piece), jnp.bfloat16),
            pltpu.VMEM((3, 8, ch), jnp.float32),
            pltpu.VMEM((modes, ch), jnp.float32),
            pltpu.VMEM((modes, ch), jnp.float32),
            pltpu.VMEM((modes, ch), jnp.float32),
            pltpu.SemaphoreType.DMA((2,)),
            pltpu.SemaphoreType.DMA((count,)),
            pltpu.SemaphoreType.DMA((count,)),
            pltpu.SemaphoreType.DMA((count,)),
            pltpu.SemaphoreType.DMA((count,)),
            pltpu.SemaphoreType.DMA((count,)),
            pltpu.SemaphoreType.DMA((2, n, count)),
            pltpu.SemaphoreType.DMA((n, count)),
            pltpu.SemaphoreType.DMA((count, contexts)),
            pltpu.SemaphoreType.DMA((count, contexts)),
            pltpu.SemaphoreType.DMA((n, count)),
            pltpu.SemaphoreType.DMA((2, n, count)),
            pltpu.SemaphoreType.DMA((count,)),
            pltpu.SemaphoreType.DMA((count,)),
        ],
        compiler_params=pltpu.CompilerParams(
            collective_id=0, has_side_effects=True, vmem_limit_bytes=56 * 1024 * 1024
        ),
        cost_estimate=pl.CostEstimate(flops=flops, bytes_accessed=9_000_000, transcendentals=0),
    )(
        tokens.T,
        in_weight.transpose(1, 2, 0),
        out_weight,
        short_filter.transpose(1, 0, 2),
        mode_weight.T,
        decay_rate.T,
    )
    return out.T


def solution(mesh):
    placed = (
        P(("groups", "context"), "tensor"),
        P(None, None, "tensor"),
        P(None, None, "tensor"),
        P("tensor", None),
        P("tensor", None),
        P("tensor", None),
    )
    return jax.shard_map(
        per_device,
        mesh=mesh,
        in_specs=placed,
        out_specs=P(("groups", "context"), "tensor"),
        check_vma=False,
    )
```
